512 devices in a mesh: wide: 32 (over z, y_lo, core), narrow: 16 (over x, y_hi).
Axes of the slice: x: 4, y: 8 (y_hi: 4, y_lo: 2; y = y_hi * 2 + y_lo), z: 8, core: 2. Of those that a mesh axis runs over, the one named last changes fastest.
Arguments:
- tokens: bfloat16 [4096, 4096], P('narrow'), may hold values from -6 to 6
- gate_matrix: bfloat16 [4096, 16384], P('narrow', 'wide'), may hold values from -0.09375 to 0.09375
- up_matrix: bfloat16 [4096, 16384], P('narrow', 'wide'), may hold values from -0.09375 to 0.09375
- down_matrix: bfloat16 [16384, 4096], P('wide', 'narrow'), may hold values from -0.09375 to 0.09375
- adapter_first: bfloat16 [32, 64, 16384], P('narrow', None, 'wide'), may hold values from -0.046875 to 0.046875
- adapter_second: bfloat16 [32, 64, 4096], P('narrow', None, 'wide'), may hold values from -0.75 to 0.75
- block_slot_choice: int32 [32], replicated, may hold values from 0 to 31, as said below
- live_block_rows: int32 [32], replicated, may hold values from 32 to 128, as said below
Outputs:
- mixed: bfloat16 [4096, 4096], P('narrow', 'wide')
The draws below stay inside these ranges and needn't reach their ends.
Inputs may be any that keep to these rules, and one draw needn't show every extreme that they name: `block_slot_choice`: slots n * 2 to (n + 1) * 2 - 1 lie on index n of narrow, and each such group of slots is named by exactly 2 blocks. Rows of block b at or past live_block_rows[b] are padding.
All inputs are finite; a program needn't handle non-finite values.
Results may differ from the reference program's by a relative error of at most 0.0056.
Values may be sent and summed in bfloat16 or wider, within the bound.
A program may use at most 64 MiB of HBM per device.

```python
import jax
import jax.numpy as jnp
from jax import lax

MODEL_WIDTH = 4096
HIDDEN_COUNT = 16384
ADAPTER_RANK = 64
BLOCK = 128
SLOT_DEV = 2
BLK_DEV = 2
TOKENS = 4096
NBLOCKS = 32
ADAPTER_SLOTS = 32


def draw_block_slot_choice(key, part):
    key = jax.random.fold_in(key, 41)
    key_perm, key_slot = jax.random.split(key)
    shuffled = jax.random.permutation(key_perm, NBLOCKS)
    server = shuffled // BLK_DEV
    within = jax.random.randint(key_slot, (NBLOCKS,), 0, SLOT_DEV)
    within = jnp.where(shuffled == NBLOCKS - 1, SLOT_DEV - 1, within)
    within = jnp.where(shuffled == 0, 0, within)
    return (server * SLOT_DEV + within).astype(jnp.int32)


def draw_live_block_rows(key, part):
    key = jax.random.fold_in(key, 57)
    key_rows, key_perm = jax.random.split(key)
    counts = jax.random.randint(key_rows, (NBLOCKS,), BLOCK // 4, BLOCK + 1)
    shuffled = jax.random.permutation(key_perm, NBLOCKS)
    counts = jnp.where(shuffled == 0, BLOCK, counts)
    counts = jnp.where(shuffled == 1, BLOCK // 4, counts)
    return counts.astype(jnp.int32)


def raised(entries, own_key, source, target, shards_of, factor):
    owner, partner = [(jnp.arange(entries.shape[dim]) // (entries.shape[dim] // shards_of)).reshape([-1 if axis == dim else 1 for axis in range(entries.ndim)]) for dim in (source, target)]
    chosen = jax.random.permutation(own_key, shards_of)[partner]
    strong = (owner == chosen) | (owner == (partner + shards_of // 2) % shards_of)
    return jnp.where(strong, factor * entries, entries)


def shard_levels(own_key, shape, shards, smallest, high):
    level = 1.0
    for axis_at, parts in shards:
        heights = jax.random.uniform(jax.random.fold_in(jax.random.fold_in(own_key, 6), axis_at), (parts,), jnp.float32, smallest / len(shards), high / len(shards))
        level = level * jnp.repeat(jnp.exp(heights), shape[axis_at] // parts).reshape((-1,) + (1,) * (len(shape) - 1 - axis_at))
    return level


def noise(rng, extent, width, bound, pieces=(), kind=jnp.bfloat16):
    level = shard_levels(rng, extent, pieces, -0.22, 0.18) if pieces else 1.0
    drawn = jax.random.normal(rng, extent, jnp.float32) * width * level
    return jnp.minimum(jnp.maximum(drawn, -bound), bound).astype(kind)


def bell_draw_with(own_key, shape, scale, most, cuts, heavy, held_as=jnp.bfloat16):
    values = scale * jax.random.normal(own_key, shape, jnp.float32)
    if cuts:
        values = values * shard_levels(own_key, shape, cuts, -0.22, 0.18)
    return jnp.clip(raised(values, jax.random.fold_in(own_key, 3), *heavy), -most, most).astype(held_as)


def setup_inputs(seed: int = 0) -> dict:
    splits = jax.random.split(jax.random.key(seed), 9)
    return {
        "tokens": noise(splits[0], (TOKENS, MODEL_WIDTH), 1.0, 6.0, ((0, 16),)),
        "gate_matrix": noise(splits[1], (MODEL_WIDTH, HIDDEN_COUNT), MODEL_WIDTH ** -0.5, 0.09375, ((0, 16), (1, 32))),
        "up_matrix": noise(splits[2], (MODEL_WIDTH, HIDDEN_COUNT), MODEL_WIDTH ** -0.5, 0.09375, ((0, 16), (1, 32))),
        "down_matrix": bell_draw_with(splits[3], (HIDDEN_COUNT, MODEL_WIDTH), HIDDEN_COUNT ** -0.5, 0.09375, ((0, 32), (1, 16)), (0, 1, 32, 2.75)),
        "adapter_first": noise(splits[4], (ADAPTER_SLOTS, ADAPTER_RANK, HIDDEN_COUNT), HIDDEN_COUNT ** -0.5, 0.046875, ((0, 16), (2, 32))),
        "adapter_second": noise(splits[5], (ADAPTER_SLOTS, ADAPTER_RANK, MODEL_WIDTH), ADAPTER_RANK ** -0.5, 0.75, ((0, 16), (2, 32))),
        "block_slot_choice": draw_block_slot_choice(jax.random.fold_in(splits[8], 71), 0),
        "live_block_rows": draw_live_block_rows(jax.random.fold_in(splits[8], 71), 0),
    }


def reference(tokens, gate_matrix, up_matrix, down_matrix, adapter_first, adapter_second, block_slot_choice, live_block_rows):
    gate_values = jnp.dot(tokens, gate_matrix, preferred_element_type=jnp.float32)
    up_values = jnp.dot(tokens, up_matrix, preferred_element_type=jnp.float32)
    hidden = (jax.nn.silu(gate_values) * up_values).astype(jnp.bfloat16)
    base_out = jnp.dot(hidden, down_matrix, preferred_element_type=jnp.float32)
    blocked = hidden.reshape(NBLOCKS, BLOCK, HIDDEN_COUNT)

    def one_block(inputs):
        block_hidden, store_slot_index = inputs
        left_factor_tile = lax.dynamic_index_in_dim(adapter_first, store_slot_index, 0, keepdims=False)
        right_factor_tile = lax.dynamic_index_in_dim(adapter_second, store_slot_index, 0, keepdims=False)
        low_rank = jnp.dot(block_hidden, left_factor_tile.T, preferred_element_type=jnp.float32)
        low_rounded = low_rank.astype(jnp.bfloat16)
        return jnp.dot(low_rounded, right_factor_tile, preferred_element_type=jnp.float32)

    adapter_out = lax.map(one_block, (blocked, block_slot_choice)).reshape(TOKENS, MODEL_WIDTH)
    positions = jnp.arange(BLOCK, dtype=jnp.int32)
    live_rows = (positions[None, :] < live_block_rows[:, None]).reshape(TOKENS, 1)
    return jnp.where(live_rows, base_out + 2.0 * adapter_out, 0.0).astype(jnp.bfloat16)
```

```python
import functools

import jax
import jax.numpy as jnp
from jax import lax
from jax.experimental import pallas as pl
from jax.experimental.pallas import tpu as pltpu
from jax.sharding import PartitionSpec as P

MESH = pl.DeviceIdType.MESH
BF16, F32 = jnp.bfloat16, jnp.float32
BLOCK = 128
RANK = 64
X, Y, Z = 4, 8, 8
GATE, UP, FIRST, SECOND, DOWN = range(5)


def place(x, y, z, core):
    return {"narrow": x * 4 + y // 2, "wide": z * 4 + (y % 2) * 2 + core}


def kernel(
    slots, live, tokens, gate, up, down, first, second, out,
    gbuf, ubuf, dbuf, abuf, bbuf, tok, gacc, uacc, hid,
    own, xsend, xrecv, zsend, zrecv, lxs, lxr, lzs, lzr, fsend, frecv,
    ws, wr, rs, ss, sr, ts, tr, tf, xss, xrs, zss, zrs, lxss, lxrs, lzss, lzrs, fss, frs,
):
    n = lax.axis_index("narrow")
    w = lax.axis_index("wide")
    x, yh = n // 4, n % 4
    z, yl, core = w // 4, (w // 2) % 2, w % 2
    y = yh * 2 + yl
    tx = yl + 2 * core
    role = tx * 4 + yh
    rel = (x - tx + 4) % 4

    def copy(src, dst, send, recv, dev):
        return pltpu.make_async_remote_copy(
            src_ref=src, dst_ref=dst, send_sem=send, recv_sem=recv, device_id=dev, device_id_type=MESH
        )

    def arrived(dst, recv):
        copy(dst, dst, recv, recv, place(x, y, z, 1 - core)).wait_recv()

    def sent(src, send):
        copy(src, src, send, send, place(x, y, z, 1 - core)).wait_send()

    barrier = pltpu.get_barrier_semaphore()
    partners = []
    for dx in range(X):
        for dy in range(2):
            for dc in range(2):
                if dx or dy or dc:
                    partners.append(place((x + dx) % 4, yh * 2 + (yl + dy) % 2, z, (core + dc) % 2))
    partners.append(place(x, (y + 2 * yl - 1 + 8) % 8, z, core))
    for dz in range(1, Z):
        partners.append(place(x, y, (z + dz) % 8, core))
    for partner in partners:
        pl.semaphore_signal(barrier, inc=1, device_id=partner, device_id_type=MESH)
    pl.semaphore_wait(barrier, len(partners))

    bufs = (gbuf, ubuf, abuf, bbuf, dbuf)

    def chunk(m, c, k, ys):
        if m == SECOND:
            return bbuf.at[c, ys, k]
        return bufs[m].at[c + 2 * k, ys]

    def spread_one(m, e, dx, dy, src, dst, recv, go):
        stays = (dx == x) & (x % 2 == core) & (dy == y)
        if go:
            @pl.when(stays)
            def _():
                pltpu.make_async_copy(src, dst, recv).start()

            @pl.when(jnp.logical_not(stays))
            def _():
                copy(src, dst, ws.at[m, e], recv, place(dx, dy, z, x % 2)).start()
        else:
            @pl.when(jnp.logical_not(stays))
            def _():
                sent(src, ws.at[m, e])

    def spread(m, go=True):
        k = x // 2
        for e in range(2):
            if m == SECOND:
                dy = yh * 2 + (yl + k) % 2
                spread_one(m, e, yl + 2 * core, dy, second.at[e], bbuf.at[x % 2, dy, e], wr.at[m, e, dy], go)
                continue
            if m == DOWN:
                src = down.at[pl.ds(e * 256, 256), :]
            elif m == FIRST:
                src = first.at[:, :, pl.ds(e * 256, 256)]
            else:
                src = (gate, up)[m].at[:, pl.ds(e * 256, 256)]
            spread_one(m, e, 2 * core + e, y, src, bufs[m].at[x, y], wr.at[m, k, y], go)

    def at_step(k, t):
        return (y - t + 8) % 8 if k == 0 else (y + t) % 8

    def pass_on(m, t, last=False):
        for k in range(2):
            ys = at_step(k, t)
            ref, recv = chunk(m, core, k, ys), wr.at[m, k, ys]
            arrived(ref, recv)
            if not last:
                to = (y + 1) % 8 if k == 0 else (y + 7) % 8
                copy(ref, ref, rs.at[m, k, ys], recv, place(x, to, z, core)).start()
            copy(ref, ref, ss.at[m, k, ys], sr.at[m, k, ys], place(x, y, z, 1 - core)).start()

    def from_sibling(m, t):
        for k in range(2):
            ys = at_step(k, t)
            arrived(chunk(m, 1 - core, k, ys), sr.at[m, k, ys])

    def token_copy(g, src, send, dx, dc):
        return copy(src, tok.at[g], send, tr.at[g], place((x + dx + 4) % 4, y, z, dc))

    holds = x % 2 == yl
    held_by = (x - yl + 4) % 4 // 2

    def send_tokens(go=True):
        for g in range(4):
            src = tokens.at[:, pl.ds(g * 1024, 1024)]
            if go:
                @pl.when(holds)
                def _():
                    token_copy(g, src, ts.at[g], 1 - 2 * core, held_by).start()

                @pl.when(rel == 0)
                def _():
                    pltpu.make_async_copy(src, tok.at[g], tr.at[g]).start()
            else:
                @pl.when(holds)
                def _():
                    sent(src, ts.at[g])

    def forwards(g):
        return ((rel == 1) & (g % 2 == 0)) | ((rel == 3) & (g % 2 == 1))

    def take_tokens(g):
        arrived(tok.at[g], tr.at[g])

        @pl.when(forwards(g))
        def _():
            token_copy(g, tok.at[g], tf.at[g], 2 - rel, core).start()

    def multiply(t):
        for m in (GATE, UP):
            from_sibling(m, t)
        for k in range(2):
            ys = at_step(k, t)
            p, i = ys % 2, ys // 2
            cols = pl.ds(pl.multiple_of(i * 256, 256), 256)
            for m, acc in ((GATE, gacc), (UP, uacc)):
                total = acc[p]
                for c in range(2):
                    total += jnp.dot(tok[c + 2 * k, :, cols], bufs[m][c + 2 * k, ys], preferred_element_type=F32)
                acc[p] = total

    spread(GATE)
    spread(UP)
    gacc[...] = jnp.zeros_like(gacc)
    uacc[...] = jnp.zeros_like(uacc)
    pass_on(GATE, 0)
    pass_on(UP, 0)
    send_tokens()

    @pl.loop(1, 5)
    def _(t):
        pass_on(GATE, t)
        pass_on(UP, t)
        take_tokens(t - 1)

    spread(FIRST)
    spread(SECOND)
    spread(DOWN)

    @pl.loop(5, 7)
    def _(t):
        pass_on(GATE, t)
        pass_on(UP, t)
        multiply(2 * t - 10)
        multiply(2 * t - 9)

    pass_on(FIRST, 0)
    pass_on(SECOND, 0)
    multiply(4)
    pass_on(GATE, 7, last=True)
    pass_on(UP, 7, last=True)
    multiply(5)
    pass_on(FIRST, 1)
    pass_on(SECOND, 1)
    multiply(6)
    multiply(7)
    for p in range(2):
        hid[:, p * 256:(p + 1) * 256] = (jax.nn.silu(gacc[p]) * uacc[p]).astype(BF16)

    @pl.loop(2, 7)
    def _(t):
        pass_on(FIRST, t)
        pass_on(SECOND, t)

    pass_on(DOWN, 0)
    pass_on(FIRST, 7, last=True)
    pass_on(SECOND, 7, last=True)

    @pl.loop(0, 8)
    def _(t):
        from_sibling(FIRST, t)
        from_sibling(SECOND, t)

    low = []
    chosen = []
    for b in range(2):
        s = slots[role * 2 + b]
        chosen.append(s)
        part = jnp.zeros((BLOCK, RANK), F32)
        for p in range(2):
            row = (s // 8) * 16 + ((s // 2) % 4) * 4 + 2 * p + s % 2
            part += lax.dot_general(
                hid[b * BLOCK:(b + 1) * BLOCK, p * 256:(p + 1) * 256],
                abuf[row // 16, (row // 2) % 8, row % 2],
                (((1,), (1,)), ((), ())),
                preferred_element_type=F32,
            )
        low.append(part)
    lxs[...] = jnp.concatenate(low, axis=1)

    def low_x(dx):
        return copy(lxs, lxr.at[x], lxss.at[dx], lxrs.at[x], place((x + dx) % 4, y, z, core))

    def low_z(dz):
        return copy(lzs, lzr.at[z], lzss.at[dz], lzrs.at[z], place(x, y, (z + dz) % 8, core))

    for dx in range(1, X):
        low_x(dx).start()

    def ready(k, t):
        first_odd = yl if k == 0 else 1 - yl
        return (t == 7) | ((t > 0) & (t % 2 == first_odd))

    def group(k, q):
        first_odd = yl if k == 0 else 1 - yl
        if k == 0:
            return (yh + first_odd - 1 - q + 8) % 4
        return (yh + 1 - first_odd + q) % 4

    def to_x(f, dst):
        return copy(xsend.at[f, dst], xrecv.at[f, x], xss.at[f, dst], xrs.at[f, x], place(dst, y, z, core))

    def to_z(f):
        return copy(zsend.at[f], zrecv.at[z], zss.at[f], zrs.at[z], place(x, y, f, core))

    def project(k, i):
        for c in range(2):
            xs = c + 2 * k
            part = jnp.dot(hid[:, :256], dbuf[xs, 2 * i], preferred_element_type=F32)
            part += jnp.dot(hid[:, 256:], dbuf[xs, 2 * i + 1], preferred_element_type=F32)
            f = 2 * xs + i // 2
            for h in range(2):
                dst = i % 2 + 2 * h
                half = part[:, h * 128:(h + 1) * 128]

                @pl.when(dst == x)
                def _():
                    own[f] = half

                @pl.when(dst != x)
                def _():
                    xsend[f, dst] = half.astype(BF16)
                    to_x(f, dst).start()

    def combine(k, i):
        @pl.when(i % 2 == x % 2)
        def _():
            for c in range(2):
                f = 2 * (c + 2 * k) + i // 2
                total = own[f]
                for dx in range(1, X):
                    src = (x + dx) % 4
                    arrived(xrecv.at[f, src], xrs.at[f, src])
                    total += xrecv[f, src].astype(F32)

                @pl.when(f == z)
                def _():
                    own[f] = total

                @pl.when(f != z)
                def _():
                    zsend[f] = total.astype(BF16)
                    to_z(f).start()

    def down_step(t, last=False):
        pass_on(DOWN, t, last)
        from_sibling(DOWN, t)
        for k in range(2):
            @pl.when(ready(k, t))
            def _():
                first_odd = yl if k == 0 else 1 - yl
                q = (t - 1) // 2 + jnp.where((t == 7) & (first_odd == 0), 0, 0)
                project(k, group(k, q))

                @pl.when(q > 0)
                def _():
                    combine(k, group(k, q + 3))

    from_sibling(DOWN, 0)

    @pl.loop(1, 3)
    def _(t):
        down_step(t)

    total = lxs[...]
    for dx in range(1, X):
        src = (x + dx) % 4
        arrived(lxr.at[src], lxrs.at[src])
        total += lxr[src]
    lzs[...] = total
    for dz in range(1, Z):
        low_z(dz).start()

    @pl.loop(3, 7)
    def _(t):
        down_step(t)

    down_step(7, last=True)
    for k in range(2):
        combine(k, group(k, 3))

    total = lzs[...]
    for dz in range(1, Z):
        src = (z + dz) % 8
        arrived(lzr.at[src], lzrs.at[src])
        total += lzr[src]
    low_rounded = total.astype(BF16)
    lora = []
    for b in range(2):
        s = chosen[b]
        r = s // 16
        xs, i, u = s // 8, (s // 2) % 4, s % 2
        ys = 2 * i + (r + x) % 2
        lora.append(jnp.dot(low_rounded[:, b * RANK:(b + 1) * RANK], bbuf[xs % 2, ys, u], preferred_element_type=F32))

    total = own[z]
    for dz in range(1, Z):
        src = (z + dz) % 8
        arrived(zrecv.at[src], zrs.at[src])
        total += zrecv[src].astype(F32)
    total += 2.0 * jnp.concatenate(lora, axis=0)
    row = lax.broadcasted_iota(jnp.int32, (2 * BLOCK, BLOCK), 0)
    limit = jnp.where(row < BLOCK, live[role * 2], BLOCK + live[role * 2 + 1])
    mixed = jnp.where(row < limit, total, 0.0).astype(BF16)

    stays = tx == x
    back = copy(fsend, frecv, fss, frs, place(tx, yh * 2 + x % 2, z, x // 2))

    @pl.when(stays)
    def _():
        out[...] = mixed

    @pl.when(jnp.logical_not(stays))
    def _():
        fsend[...] = mixed
        back.start()

    for m in range(5):
        spread(m, go=False)
    send_tokens(go=False)
    for g in range(4):
        @pl.when(forwards(g))
        def _():
            sent(tok.at[g], tf.at[g])

    @pl.loop(0, 8)
    def _(t):
        for m in range(5):
            for k in range(2):
                ys = at_step(k, t)
                ref = chunk(m, core, k, ys)

                @pl.when(t < 7)
                def _():
                    sent(ref, rs.at[m, k, ys])

                sent(ref, ss.at[m, k, ys])

    for dx in range(1, X):
        sent(lxs, lxss.at[dx])
        dst = (x + dx) % 4
        for f in range(8):
            sent(xsend.at[f, dst], xss.at[f, dst])
    for dz in range(1, Z):
        sent(lzs, lzss.at[dz])
        f = (z + dz) % 8
        sent(zsend.at[f], zss.at[f])

    @pl.when(jnp.logical_not(stays))
    def _():
        arrived(frecv, frs)
        out[...] = frecv[...]
        sent(fsend, fss)


def local(tokens, gate, up, down, first, second, slots, live):
    dma = pltpu.SemaphoreType.DMA
    smem = pl.BlockSpec(memory_space=pltpu.SMEM)
    hbm = pl.BlockSpec(memory_space=pl.ANY)
    return pl.pallas_call(
        kernel,
        out_shape=jax.ShapeDtypeStruct((256, 128), BF16),
        in_specs=[smem, smem] + [hbm] * 6,
        out_specs=pl.BlockSpec(memory_space=pltpu.VMEM),
        scratch_shapes=[
            pltpu.VMEM((4, 8, 256, 256), BF16),
            pltpu.VMEM((4, 8, 256, 256), BF16),
            pltpu.VMEM((4, 8, 256, 256), BF16),
            pltpu.VMEM((4, 8, 2, RANK, 256), BF16),
            pltpu.VMEM((2, 8, 2, RANK, 128), BF16),
            pltpu.VMEM((4, 256, 1024), BF16),
            pltpu.VMEM((2, 256, 256), F32),
            pltpu.VMEM((2, 256, 256), F32),
            pltpu.VMEM((256, 512), BF16),
            pltpu.VMEM((8, 256, 128), F32),
            pltpu.VMEM((8, 4, 256, 128), BF16),
            pltpu.VMEM((8, 4, 256, 128), BF16),
            pltpu.VMEM((8, 256, 128), BF16),
            pltpu.VMEM((8, 256, 128), BF16),
            pltpu.VMEM((128, 128), F32),
            pltpu.VMEM((4, 128, 128), F32),
            pltpu.VMEM((128, 128), F32),
            pltpu.VMEM((8, 128, 128), F32),
            pltpu.VMEM((256, 128), BF16),
            pltpu.VMEM((256, 128), BF16),
            dma((5, 2)),
            dma((5, 2, 8)),
            dma((5, 2, 8)),
            dma((5, 2, 8)),
            dma((5, 2, 8)),
            dma((4,)),
            dma((4,)),
            dma((4,)),
            dma((8, 4)),
            dma((8, 4)),
            dma((8,)),
            dma((8,)),
            dma((4,)),
            dma((4,)),
            dma((8,)),
            dma((8,)),
            dma,
            dma,
        ],
        compiler_params=pltpu.CompilerParams(
            collective_id=0, has_side_effects=True, vmem_limit_bytes=48 << 20
        ),
        name="swiglu_ring",
    )(slots, live, tokens, gate, up, down, first, second)


def solution(mesh):
    in_specs = (
        P("narrow", None),
        P("narrow", "wide"),
        P("narrow", "wide"),
        P("wide", "narrow"),
        P("narrow", None, "wide"),
        P("narrow", None, "wide"),
        P(),
        P(),
    )
    return jax.shard_map(local, mesh=mesh, in_specs=in_specs, out_specs=P("narrow", "wide"), check_vma=False)
```

```python
import jax
import jax.numpy as jnp
from jax import lax
from jax.experimental import pallas as pl
from jax.experimental.pallas import tpu as pltpu
from jax.sharding import PartitionSpec as P

MESH = pl.DeviceIdType.MESH
BF16, F32 = jnp.bfloat16, jnp.float32
BLOCK = 128
RANK = 64
X, Y, Z = 4, 8, 8
GATE, UP, FIRST, SECOND, DOWN, DOWN2 = range(6)


def place(x, y, z, core):
    return {"narrow": x * 4 + y // 2, "wide": z * 4 + (y % 2) * 2 + core}


def kernel(
    slots, live, tokens, gate, up, down, first, second, out,
    gbuf, ubuf, dbuf, abuf, bbuf, tok, gacc, uacc, hs, hid,
    own, xsend, xrecv, zsend, zrecv, lxs, lxr, lzs, lzr, lows, fsend, frecv,
    ws, wr, gs, rs, ss, sr, ts, tr, tz, tn, hss, hr, xss, xrs, zss, zrs, lxss, lxrs, lzss, lzrs, lbss, lbrs, fss, frs,
):
    n = lax.axis_index("narrow")
    w = lax.axis_index("wide")
    x, yh = n // 4, n % 4
    z, yl, core = w // 4, (w // 2) % 2, w % 2
    y = yh * 2 + yl
    tx = yl + 2 * core
    role = tx * 4 + yh

    def copy(src, dst, send, recv, dev):
        return pltpu.make_async_remote_copy(
            src_ref=src, dst_ref=dst, send_sem=send, recv_sem=recv, device_id=dev, device_id_type=MESH
        )

    def arrived(dst, recv):
        copy(dst, dst, recv, recv, place(x, y, z, 1 - core)).wait_recv()

    def sent(src, send):
        copy(src, src, send, send, place(x, y, z, 1 - core)).wait_send()

    barrier = pltpu.get_barrier_semaphore()
    partners = [place(x, (y + dy) % 8, z, (core + dc) % 2) for dy in range(Y) for dc in range(2) if dy or dc]
    for dx in range(1, X):
        for dc in range(2):
            for dy in range(2):
                partners.append(place((x + dx) % 4, yh * 2 + (yl + dy) % 2, z, (core + dc) % 2))
    for dz in range(1, Z):
        partners.append(place(x, y, (z + dz) % 8, core))
    for partner in partners:
        pl.semaphore_signal(barrier, inc=1, device_id=partner, device_id_type=MESH)
    own_hid = (yh == x) & (yl == x % 2) & (core == x // 2)
    for p in range(2):
        @pl.when(jnp.logical_not(own_hid & (p == 1 - yl)))
        def _():
            pl.semaphore_signal(barrier, inc=1, device_id=place(tx, 2 * x + 1 - p, z, yh // 2), device_id_type=MESH)
    pl.semaphore_wait(barrier, len(partners) + 2 - jnp.where(own_hid, 1, 0))

    bufs = (gbuf, ubuf, abuf, bbuf)

    def chunk(m, c, k, ys):
        if m == SECOND:
            return bbuf.at[c, ys, k]
        if m >= DOWN:
            return dbuf.at[c + 2 * k, ys, pl.ds((m - DOWN) * 128, 128)]
        return bufs[m].at[c + 2 * k, ys]

    def spread_one(m, e, dx, dy, src, dst, recv, go):
        stays = (dx == x) & (x % 2 == core) & (dy == y)
        if go:
            @pl.when(stays)
            def _():
                pltpu.make_async_copy(src, dst, recv).start()

            @pl.when(jnp.logical_not(stays))
            def _():
                copy(src, dst, ws.at[m, e], recv, place(dx, dy, z, x % 2)).start()
        else:
            @pl.when(jnp.logical_not(stays))
            def _():
                sent(src, ws.at[m, e])

    def spread(m, go=True):
        k = x // 2
        for e in range(2):
            if m == SECOND:
                dy = yh * 2 + (yl + k) % 2
                spread_one(m, e, yl + 2 * core, dy, second.at[e], bbuf.at[x % 2, dy, e], wr.at[m, e, dy], go)
                continue
            if m >= DOWN:
                h = (m - DOWN) * 128
                src = down.at[pl.ds(e * 256 + h, 128), :]
                dst = dbuf.at[x, y, pl.ds(h, 128)]
                spread_one(m, e, 2 * core + e, y, src, dst, wr.at[m, k, y], go)
                continue
            src = first.at[:, :, pl.ds(e * 256, 256)]
            spread_one(m, e, 2 * core + e, y, src, bufs[m].at[x, y], wr.at[m, k, y], go)

    def at_step(k, t):
        return (y - t + 8) % 8 if k == 0 else (y + t) % 8

    def pass_on(m, t, last=False):
        for k in range(2):
            ys = at_step(k, t)
            ref, recv = chunk(m, core, k, ys), wr.at[m, k, ys]
            arrived(ref, recv)
            to = (y + 1) % 8 if k == 0 else (y + 7) % 8

            def onward():
                copy(ref, ref, rs.at[m], recv, place(x, to, z, core)).start()

            if last is False:
                onward()
            elif last is not True:
                pl.when(jnp.logical_not(last))(onward)
            copy(ref, ref, ss.at[m], sr.at[m, k, ys], place(x, y, z, 1 - core)).start()

    def from_sibling(m, t):
        for k in range(2):
            ys = at_step(k, t)
            arrived(chunk(m, 1 - core, k, ys), sr.at[m, k, ys])

    def deal(m):
        src = (gate, up)[m]
        for e in range(2):
            to = place(x, 2 * (2 * core + e) + 1 - yl, z, yh // 2)
            copy(src.at[:, pl.ds(e * 256, 256)], bufs[m].at[4 * x + yh], gs.at[m], wr.at[m, yh % 2, x], to).start()

    def circulate(m, dx):
        xs = (x + dx + 4) % 4
        for k in range(2):
            ref, recv = bufs[m].at[4 * xs + 2 * core + k], wr.at[m, k, xs]
            arrived(ref, recv)
            for way in (1, -1):
                if dx == 0 or (dx == -way and way == 1 - 2 * k):
                    copy(ref, ref, rs.at[m], recv, place((x + way + 4) % 4, y, z, core)).start()
            copy(ref, ref, ss.at[m], sr.at[m, k, xs], place(x, y, z, 1 - core)).start()

    def weights_from_sibling(m):
        for xs in range(4):
            for k in range(2):
                arrived(bufs[m].at[4 * xs + 2 * (1 - core) + k], sr.at[m, k, xs])

    def deal_tokens():
        src = tokens.at[:, pl.ds(pl.multiple_of(z * 512 + core * 256, 256), 256)]
        for step in range(1, 4):
            to = place(x, (y + step * (2 * yl - 1) + 8) % 8, z, yh // 2)
            copy(src, tok.at[yh % 2, z, core], ts, tr.at[yh % 2, z, core], to).start()

    def held(k):
        return yh == 2 * core + k

    def keep_tokens():
        @pl.when(core == yh // 2)
        def _():
            for part in range(16):
                src = tokens.at[:, pl.ds(part * 256, 256)]
                pltpu.make_async_copy(src, tok.at[yh % 2, part // 2, part % 2], tn).start()

    def tokens_kept():
        @pl.when(core == yh // 2)
        def _():
            pltpu.make_async_copy(tok.at[yh % 2], tok.at[yh % 2], tn).wait()

    def token_step(d):
        for k in range(2):
            @pl.when(jnp.logical_not(held(k)))
            def _():
                for way in (1, -1):
                    reach = 4 if way == 1 - 2 * k else 3
                    if d > reach or (d == 0 and way == -1):
                        continue
                    zs = (z - way * d + 8) % 8
                    for h in range(2):
                        ref, recv = tok.at[k, zs, h], tr.at[k, zs, h]
                        arrived(ref, recv)
                        for onward in (1, -1) if d == 0 else (way,):
                            if d < reach or d == 0:
                                copy(ref, ref, tz.at[k], recv, place(x, y, (z + onward + 8) % 8, core)).start()

    def multiply(zs):
        for k in range(2):
            for m, acc in ((GATE, gacc), (UP, uacc)):
                total = acc[k]
                for h in range(2):
                    total += jnp.dot(tok[k, zs, h], bufs[m][2 * zs + h], preferred_element_type=F32)
                acc[k] = total

    def pass_hidden():
        for k in range(2):
            hs[k] = (jax.nn.silu(gacc[k]) * uacc[k]).astype(BF16)
            stays = own_hid & (k == x % 2)
            src, dst, recv = hs.at[k], hid.at[1 - yl], hr.at[1 - yl]

            @pl.when(stays)
            def _():
                pltpu.make_async_copy(src, dst, recv).start()

            @pl.when(jnp.logical_not(stays))
            def _():
                copy(src, dst, hss.at[k], recv, place(yh, 4 * core + 2 * k + x % 2, z, x // 2)).start()

    def adapters(t, last=False):
        pass_on(FIRST, t, last)
        pass_on(SECOND, t, last)

    def down_step(t, last=False):
        pass_on(DOWN, t, last)
        pass_on(DOWN2, t, last)

    deal_tokens()
    for m in (FIRST, SECOND, DOWN, DOWN2):
        spread(m)
    keep_tokens()
    gacc[...] = jnp.zeros_like(gacc)
    uacc[...] = jnp.zeros_like(uacc)
    token_step(0)
    deal(GATE)
    deal(UP)
    circulate(GATE, 0)
    adapters(0)
    token_step(1)
    circulate(UP, 0)
    adapters(1)
    down_step(0)
    circulate(GATE, -1)
    circulate(GATE, 1)
    adapters(2)
    circulate(UP, -1)
    circulate(UP, 1)
    down_step(1)
    adapters(3)
    token_step(2)
    adapters(4)
    down_step(2)
    for m in (GATE, UP):
        circulate(m, 2)
    adapters(5)
    for m in (GATE, UP):
        weights_from_sibling(m)
    tokens_kept()
    multiply(z)
    adapters(6)
    down_step(3)
    multiply((z + 1) % 8)
    multiply((z + 7) % 8)
    token_step(3)
    adapters(7, last=True)
    multiply((z + 2) % 8)
    multiply((z + 6) % 8)
    multiply((z + 3) % 8)
    multiply((z + 5) % 8)
    token_step(4)
    multiply((z + 4) % 8)
    pass_hidden()
    down_step(4)
    for t in range(8):
        from_sibling(FIRST, t)
        from_sibling(SECOND, t)
    down_step(5)
    for p in range(2):
        arrived(hid.at[p], hr.at[p])

    chosen = [slots[role * 2 + b] for b in range(2)]

    def quarter(i):
        return pl.ds(pl.multiple_of(i * 32, 32), 32)

    def low_x(dst):
        return copy(lxs.at[quarter(dst)], lxr.at[x], lxss, lxrs.at[x], place(dst, y, z, core))

    def low_z(dz):
        return copy(lzs, lzr.at[z], lzss, lzrs.at[z], place(x, y, (z + dz) % 8, core))

    def low_back(dst):
        part = lows.at[quarter(x)]
        return copy(part, part, lbss, lbrs.at[x], place(dst, y, z, core))

    def low_terms():
        low = []
        for b in range(2):
            s = chosen[b]
            part = jnp.zeros((BLOCK, RANK), F32)
            for p in range(2):
                row = (s // 8) * 16 + ((s // 2) % 4) * 4 + 2 * p + s % 2
                part += lax.dot_general(
                    hid[p, b * BLOCK:(b + 1) * BLOCK, :],
                    abuf[row // 16, (row // 2) % 8, row % 2],
                    (((1,), (1,)), ((), ())),
                    preferred_element_type=F32,
                )
            low.append(part)
        lxs[...] = jnp.concatenate(low, axis=1)
        for dx in range(1, X):
            low_x((x + dx) % 4).start()

    def low_over_x():
        total = lxs[quarter(x)]
        for dx in range(1, X):
            src = (x + dx) % 4
            arrived(lxr.at[src], lxrs.at[src])
            total += lxr[src]
        lzs[...] = total
        for dz in range(1, Z):
            low_z(dz).start()

    def low_over_z():
        total = lzs[...]
        for dz in range(1, Z):
            src = (z + dz) % 8
            arrived(lzr.at[src], lzrs.at[src])
            total += lzr[src]
        lows[quarter(x)] = total.astype(BF16)
        for dx in range(1, X):
            low_back((x + dx) % 4).start()

    def ready(k, t):
        first_odd = yl if k == 0 else 1 - yl
        return (t == 7) | ((t > 0) & (t % 2 == first_odd))

    def group(k, q):
        first_odd = yl if k == 0 else 1 - yl
        if k == 0:
            return (yh + first_odd - 1 - q + 8) % 4
        return (yh + 1 - first_odd + q) % 4

    def to_x(f, dst):
        return copy(xsend.at[f, dst], xrecv.at[f, x], xss, xrs.at[f, x], place(dst, y, z, core))

    def to_z(f):
        return copy(zsend.at[f], zrecv.at[z], zss, zrs.at[z], place(x, y, f, core))

    def project(k, i):
        for c in range(2):
            xs = c + 2 * k
            part = jnp.dot(hid[0], dbuf[xs, 2 * i], preferred_element_type=F32)
            part += jnp.dot(hid[1], dbuf[xs, 2 * i + 1], preferred_element_type=F32)
            f = 2 * xs + i // 2
            for h in range(2):
                dst = i % 2 + 2 * h
                half = part[:, h * 128:(h + 1) * 128]

                @pl.when(dst == x)
                def _():
                    own[f] = half

                @pl.when(dst != x)
                def _():
                    xsend[f, dst] = half.astype(BF16)
                    to_x(f, dst).start()

    def combine(k, i):
        @pl.when(i % 2 == x % 2)
        def _():
            for c in range(2):
                f = 2 * (c + 2 * k) + i // 2
                total = own[f]
                for dx in range(1, X):
                    src = (x + dx) % 4
                    arrived(xrecv.at[f, src], xrs.at[f, src])
                    total += xrecv[f, src].astype(F32)

                @pl.when(f == z)
                def _():
                    own[f] = total

                @pl.when(f != z)
                def _():
                    zsend[f] = total.astype(BF16)
                    to_z(f).start()

    def use_down(t):
        from_sibling(DOWN, t)
        from_sibling(DOWN2, t)
        for k in range(2):
            @pl.when(ready(k, t))
            def _():
                q = (t - 1) // 2
                project(k, group(k, q))

                @pl.when(q > 0)
                def _():
                    combine(k, group(k, q + 3))

    low_terms()

    @pl.loop(0, 3)
    def _(t):
        use_down(t)

    down_step(6)
    use_down(3)
    low_over_x()
    down_step(7, last=True)
    use_down(4)
    use_down(5)
    low_over_z()
    use_down(6)
    use_down(7)
    for k in range(2):
        combine(k, group(k, 3))

    for m in range(6):
        if m <= UP:
            sent(bufs[m].at[pl.ds(0, 2)], gs.at[m])
            sent(bufs[m].at[pl.ds(0, 6)], rs.at[m])
            sent(bufs[m].at[pl.ds(0, 8)], ss.at[m])
            continue
        spread(m, go=False)
        if m == SECOND:
            onward, across = bbuf.at[0, pl.ds(0, 7)], bbuf.at[0]
        elif m >= DOWN:
            rows = pl.ds(0, 128)
            onward, across = dbuf.at[pl.ds(0, 2), pl.ds(0, 7), rows], dbuf.at[pl.ds(0, 2), :, rows]
        else:
            onward, across = bufs[m].at[pl.ds(0, 2), pl.ds(0, 7)], bufs[m].at[pl.ds(0, 2)]
        sent(onward, rs.at[m])
        sent(across, ss.at[m])
    sent(tok.at[0, pl.ds(0, 3), 0], ts)
    for k in range(2):
        pl.when(jnp.logical_not(held(k)))(lambda k=k: sent(tok.at[k, pl.ds(0, 7)], tz.at[k]))
        pl.when(jnp.logical_not(own_hid & (k == x % 2)))(lambda k=k: sent(hs.at[k], hss.at[k]))
    sent(lxr.at[pl.ds(0, 3)], lxss)
    sent(lzr.at[pl.ds(0, 7)], lzss)
    sent(lows.at[pl.ds(0, 96)], lbss)
    sent(xsend.at[:, pl.ds(0, 3)], xss)

    for dx in range(1, X):
        src = (x + dx) % 4
        arrived(lows.at[quarter(src)], lbrs.at[src])
    low_rounded = lows[...]
    lora = []
    for b in range(2):
        s = chosen[b]
        r = s // 16
        xs, i, u = s // 8, (s // 2) % 4, s % 2
        ys = 2 * i + (r + x) % 2
        lora.append(jnp.dot(low_rounded[:, b * RANK:(b + 1) * RANK], bbuf[xs % 2, ys, u], preferred_element_type=F32))

    total = own[z]
    for dz in range(1, Z):
        src = (z + dz) % 8
        arrived(zrecv.at[src], zrs.at[src])
        total += zrecv[src].astype(F32)
    total += 2.0 * jnp.concatenate(lora, axis=0)
    row = lax.broadcasted_iota(jnp.int32, (2 * BLOCK, BLOCK), 0)
    limit = jnp.where(row < BLOCK, live[role * 2], BLOCK + live[role * 2 + 1])
    mixed = jnp.where(row < limit, total, 0.0).astype(BF16)

    stays = tx == x
    back = copy(fsend, frecv, fss, frs, place(tx, yh * 2 + x % 2, z, x // 2))

    @pl.when(stays)
    def _():
        out[...] = mixed

    @pl.when(jnp.logical_not(stays))
    def _():
        fsend[...] = mixed
        back.start()

    sent(zsend.at[pl.ds(0, 7)], zss)

    @pl.when(jnp.logical_not(stays))
    def _():
        arrived(frecv, frs)
        out[...] = frecv[...]
        sent(fsend, fss)


def local(tokens, gate, up, down, first, second, slots, live):
    dma = pltpu.SemaphoreType.DMA
    smem = pl.BlockSpec(memory_space=pltpu.SMEM)
    hbm = pl.BlockSpec(memory_space=pl.ANY)
    return pl.pallas_call(
        kernel,
        out_shape=jax.ShapeDtypeStruct((256, 128), BF16),
        in_specs=[smem, smem] + [hbm] * 6,
        out_specs=pl.BlockSpec(memory_space=pltpu.VMEM),
        scratch_shapes=[
            pltpu.VMEM((16, 256, 256), BF16),
            pltpu.VMEM((16, 256, 256), BF16),
            pltpu.VMEM((4, 8, 256, 256), BF16),
            pltpu.VMEM((4, 8, 2, RANK, 256), BF16),
            pltpu.VMEM((2, 8, 2, RANK, 128), BF16),
            pltpu.VMEM((2, 8, 2, 256, 256), BF16),
            pltpu.VMEM((2, 256, 256), F32),
            pltpu.VMEM((2, 256, 256), F32),
            pltpu.VMEM((2, 256, 256), BF16),
            pltpu.VMEM((2, 256, 256), BF16),
            pltpu.VMEM((8, 256, 128), F32),
            pltpu.VMEM((8, 4, 256, 128), BF16),
            pltpu.VMEM((8, 4, 256, 128), BF16),
            pltpu.VMEM((8, 256, 128), BF16),
            pltpu.VMEM((8, 256, 128), BF16),
            pltpu.VMEM((128, 128), F32),
            pltpu.VMEM((4, 32, 128), F32),
            pltpu.VMEM((32, 128), F32),
            pltpu.VMEM((8, 32, 128), F32),
            pltpu.VMEM((128, 128), BF16),
            pltpu.VMEM((256, 128), BF16),
            pltpu.VMEM((256, 128), BF16),
            dma((6, 2)),
            dma((6, 2, 8)),
            dma((2,)),
            dma((6,)),
            dma((6,)),
            dma((6, 2, 8)),
            dma(()),
            dma((2, 8, 2)),
            dma((2,)),
            dma(()),
            dma((2,)),
            dma((2,)),
            dma(()),
            dma((8, 4)),
            dma(()),
            dma((8,)),
            dma(()),
            dma((4,)),
            dma(()),
            dma((8,)),
            dma(()),
            dma((4,)),
            dma(()),
            dma(()),
        ],
        compiler_params=pltpu.CompilerParams(
            collective_id=0, has_side_effects=True, vmem_limit_bytes=60 << 20
        ),
        name="swiglu_mesh",
    )(slots, live, tokens, gate, up, down, first, second)


def solution(mesh):
    in_specs = (
        P("narrow", None),
        P("narrow", "wide"),
        P("narrow", "wide"),
        P("wide", "narrow"),
        P("narrow", None, "wide"),
        P("narrow", None, "wide"),
        P(),
        P(),
    )
    return jax.shard_map(local, mesh=mesh, in_specs=in_specs, out_specs=P("narrow", "wide"), check_vma=False)
```

```python
import jax
import jax.numpy as jnp
from jax import lax
from jax.experimental import pallas as pl
from jax.experimental.pallas import tpu as pltpu
from jax.sharding import PartitionSpec as P

MESH = pl.DeviceIdType.MESH
BF16, F32 = jnp.bfloat16, jnp.float32
BLOCK = 128
RANK = 64
X, Y, Z = 4, 8, 8
GATE, UP, FIRST, SECOND, DOWN, DOWN2 = range(6)


def place(x, y, z, core):
    return {"narrow": x * 4 + y // 2, "wide": z * 4 + (y % 2) * 2 + core}


def kernel(
    slots, live, tokens, gate, up, down, first, second, out,
    gbuf, ubuf, dbuf, abuf, bbuf, tok, gacc, uacc, hs, hid,
    own, xsend, xrecv, zsend, zrecv, lxs, lxr, lzs, lzr, lows, fsend, frecv,
    ws, wr, gs, rs, ss, sr, ts, tr, tz, tn, hss, hr, xss, xrs, zss, zrs, lxss, lxrs, lzss, lzrs, lbss, lbrs, fss, frs,
):
    n = lax.axis_index("narrow")
    w = lax.axis_index("wide")
    x, yh = n // 4, n % 4
    z, yl, core = w // 4, (w // 2) % 2, w % 2
    y = yh * 2 + yl
    tx = yl + 2 * core
    role = tx * 4 + yh
    bx = (x + 4 - z // 2) % 4

    def copy(src, dst, send, recv, dev):
        return pltpu.make_async_remote_copy(
            src_ref=src, dst_ref=dst, send_sem=send, recv_sem=recv, device_id=dev, device_id_type=MESH
        )

    def arrived(dst, recv):
        copy(dst, dst, recv, recv, place(x, y, z, 1 - core)).wait_recv()

    def sent(src, send):
        copy(src, src, send, send, place(x, y, z, 1 - core)).wait_send()

    barrier = pltpu.get_barrier_semaphore()
    partners = [place(x, (y + dy) % 8, z, (core + dc) % 2) for dy in range(Y) for dc in range(2) if dy or dc]
    for dx in range(1, X):
        for dc in range(2):
            for dy in range(2):
                partners.append(place((x + dx) % 4, yh * 2 + (yl + dy) % 2, z, (core + dc) % 2))
    for dz in range(1, Z):
        partners.append(place(x, y, (z + dz) % 8, core))
    for partner in partners:
        pl.semaphore_signal(barrier, inc=1, device_id=partner, device_id_type=MESH)
    own_hid = (yh == x) & (yl == x % 2) & (core == x // 2)
    for p in range(2):
        @pl.when(jnp.logical_not(own_hid & (p == 1 - yl)))
        def _():
            pl.semaphore_signal(barrier, inc=1, device_id=place(tx, 2 * x + 1 - p, z, yh // 2), device_id_type=MESH)
    pl.semaphore_wait(barrier, len(partners) + 2 - jnp.where(own_hid, 1, 0))

    bufs = (gbuf, ubuf, abuf, bbuf)

    def chunk(m, c, k, ys):
        if m == SECOND:
            return bbuf.at[c, ys, k]
        if m >= DOWN:
            return dbuf.at[c + 2 * k, ys, pl.ds((m - DOWN) * 128, 128)]
        return bufs[m].at[c + 2 * k, ys]

    def spread_one(m, e, dx, dy, src, dst, recv, go):
        stays = (dx == x) & (x % 2 == core) & (dy == y)
        if go:
            @pl.when(stays)
            def _():
                pltpu.make_async_copy(src, dst, recv).start()

            @pl.when(jnp.logical_not(stays))
            def _():
                copy(src, dst, ws.at[m, e], recv, place(dx, dy, z, x % 2)).start()
        else:
            @pl.when(jnp.logical_not(stays))
            def _():
                sent(src, ws.at[m, e])

    def spread(m, go=True):
        k = x // 2
        for e in range(2):
            if m == SECOND:
                dy = yh * 2 + (yl + k) % 2
                spread_one(m, e, (tx + z // 2) % 4, dy, second.at[e], bbuf.at[x % 2, dy, e], wr.at[m, e, dy], go)
                continue
            if m >= DOWN:
                h = (m - DOWN) * 128
                src = down.at[pl.ds(e * 256 + h, 128), :]
                dst = dbuf.at[x, y, pl.ds(h, 128)]
                spread_one(m, e, 2 * core + e, y, src, dst, wr.at[m, k, y], go)
                continue
            src = first.at[:, :, pl.ds(e * 256, 256)]
            spread_one(m, e, 2 * core + e, y, src, bufs[m].at[x, y], wr.at[m, k, y], go)

    def ring_step(m, d):
        for k in range(2):
            for way in (1, -1):
                reach = 4 if way == 1 - 2 * k else 3
                if d > reach or (d == 0 and way == -1):
                    continue
                ys = (y - way * d + 8) % 8
                ref, recv = chunk(m, core, k, ys), wr.at[m, k, ys]
                arrived(ref, recv)
                for onward in (1, -1) if d == 0 else (way,):
                    if d < reach:
                        copy(ref, ref, rs.at[m], recv, place(x, (y + onward + 8) % 8, z, core)).start()
                copy(ref, ref, ss.at[m], sr.at[m, k, ys], place(x, y, z, 1 - core)).start()

    def from_sibling(m, d):
        for k in range(2):
            for ys in ((y + 8 - d) % 8, (y + d) % 8)[:1 if d in (0, 4) else 2]:
                arrived(chunk(m, 1 - core, k, ys), sr.at[m, k, ys])

    def deal(m):
        src = (gate, up)[m]
        for e in range(2):
            to = place(x, 2 * (2 * core + e) + 1 - yl, z, yh // 2)
            copy(src.at[:, pl.ds(e * 256, 256)], bufs[m].at[4 * x + yh], gs.at[m], wr.at[m, yh % 2, x], to).start()

    def circulate(m, dx):
        xs = (x + dx + 4) % 4
        for k in range(2):
            ref, recv = bufs[m].at[4 * xs + 2 * core + k], wr.at[m, k, xs]
            arrived(ref, recv)
            for way in (1, -1):
                if dx == 0 or (dx == -way and way == 1 - 2 * k):
                    copy(ref, ref, rs.at[m], recv, place((x + way + 4) % 4, y, z, core)).start()
            copy(ref, ref, ss.at[m], sr.at[m, k, xs], place(x, y, z, 1 - core)).start()

    def weights_from_sibling(m):
        for xs in range(4):
            for k in range(2):
                arrived(bufs[m].at[4 * xs + 2 * (1 - core) + k], sr.at[m, k, xs])

    def rows(r):
        return pl.ds(r * BLOCK, BLOCK)

    def deal_tokens(r):
        src = tokens.at[rows(r), pl.ds(pl.multiple_of(z * 512 + core * 256, 256), 256)]
        for step in range(1, 4):
            to = place(x, (y + step * (2 * yl - 1) + 8) % 8, z, yh // 2)
            copy(src, tok.at[yh % 2, z, core, rows(r)], ts, tr.at[yh % 2, z, core, r], to).start()

    def held(k):
        return yh == 2 * core + k

    def keep_tokens():
        @pl.when(core == yh // 2)
        def _():
            for part in range(16):
                src = tokens.at[:, pl.ds(part * 256, 256)]
                pltpu.make_async_copy(src, tok.at[yh % 2, part // 2, part % 2], tn).start()

    def tokens_kept():
        @pl.when(core == yh // 2)
        def _():
            pltpu.make_async_copy(tok.at[yh % 2], tok.at[yh % 2], tn).wait()

    def token_step(d, r):
        for k in range(2):
            @pl.when(jnp.logical_not(held(k)))
            def _():
                for way in (1, -1):
                    reach = 4 if way == 1 - 2 * k else 3
                    if d > reach or (d == 0 and way == -1):
                        continue
                    zs = (z - way * d + 8) % 8
                    for h in range(2):
                        ref, recv = tok.at[k, zs, h, rows(r)], tr.at[k, zs, h, r]
                        arrived(ref, recv)
                        for onward in (1, -1) if d == 0 else (way,):
                            if d < reach or d == 0:
                                copy(ref, ref, tz.at[k], recv, place(x, y, (z + onward + 8) % 8, core)).start()

    def multiply(zs, r):
        for k in range(2):
            for m, acc in ((GATE, gacc), (UP, uacc)):
                total = acc[k, rows(r)]
                for h in range(2):
                    total += jnp.dot(tok[k, zs, h, rows(r)], bufs[m][2 * zs + h], preferred_element_type=F32)
                acc[k, rows(r)] = total

    def pass_hidden(r):
        for k in range(2):
            hs[k, rows(r)] = (jax.nn.silu(gacc[k, rows(r)]) * uacc[k, rows(r)]).astype(BF16)
            stays = own_hid & (k == x % 2)
            src, dst, recv = hs.at[k, rows(r)], hid.at[1 - yl, rows(r)], hr.at[1 - yl, r]

            @pl.when(stays)
            def _():
                pltpu.make_async_copy(src, dst, recv).start()

            @pl.when(jnp.logical_not(stays))
            def _():
                copy(src, dst, hss.at[k], recv, place(yh, 4 * core + 2 * k + x % 2, z, x // 2)).start()

    def adapters(d):
        ring_step(FIRST, d)
        ring_step(SECOND, d)

    def down_step(d):
        ring_step(DOWN, d)
        ring_step(DOWN2, d)

    def hidden_here(r):
        for p in range(2):
            arrived(hid.at[p, rows(r)], hr.at[p, r])

    chosen = [slots[role * 2 + b] for b in range(2)]

    def quarter(i):
        return pl.ds(pl.multiple_of(i * 32, 32), 32)

    def low_x(dst):
        return copy(lxs.at[quarter(dst)], lxr.at[x], lxss, lxrs.at[x], place(dst, y, z, core))

    def low_z(dz):
        return copy(lzs, lzr.at[z], lzss, lzrs.at[z], place(x, y, (z + dz) % 8, core))

    def low_back(dst):
        part = lows.at[quarter(x)]
        return copy(part, part, lbss, lbrs.at[x], place(dst, y, z, core))

    def low_terms():
        low = []
        for b in range(2):
            s = chosen[b]
            part = jnp.zeros((BLOCK, RANK), F32)
            for p in range(2):
                row = (s // 8) * 16 + ((s // 2) % 4) * 4 + 2 * p + s % 2
                part += lax.dot_general(
                    hid[p, b * BLOCK:(b + 1) * BLOCK, :],
                    abuf[row // 16, (row // 2) % 8, row % 2],
                    (((1,), (1,)), ((), ())),
                    preferred_element_type=F32,
                )
            low.append(part)
        lxs[...] = jnp.concatenate(low, axis=1)
        for dx in range(1, X):
            low_x((x + dx) % 4).start()

    def low_over_x():
        total = lxs[quarter(x)]
        for dx in range(1, X):
            src = (x + dx) % 4
            arrived(lxr.at[src], lxrs.at[src])
            total += lxr[src]
        lzs[...] = total
        for dz in range(1, Z):
            low_z(dz).start()

    def low_over_z():
        total = lzs[...]
        for dz in range(1, Z):
            src = (z + dz) % 8
            arrived(lzr.at[src], lzrs.at[src])
            total += lzr[src]
        lows[quarter(x)] = total.astype(BF16)
        for dx in range(1, X):
            low_back((x + dx) % 4).start()

    def pair(q):
        return (yh + (0, 2 * yl - 1, 1 - 2 * yl, 2)[q] + 4) % 4

    def to_x(f, dst, r):
        return copy(xsend.at[f, dst, rows(r)], xrecv.at[f, x, rows(r)], xss, xrs.at[f, x, r], place(dst, y, z, core))

    def to_z(f, r):
        return copy(zsend.at[f, rows(r)], zrecv.at[z, rows(r)], zss, zrs.at[z, r], place(x, y, f, core))

    def project(k, i, r):
        for c in range(2):
            xs = c + 2 * k
            part = jnp.dot(hid[0, rows(r)], dbuf[xs, 2 * i], preferred_element_type=F32)
            part += jnp.dot(hid[1, rows(r)], dbuf[xs, 2 * i + 1], preferred_element_type=F32)
            f = 2 * xs + i // 2
            for h in range(2):
                dst = (i % 2 + 2 * h + xs) % 4
                half = part[:, h * 128:(h + 1) * 128]

                @pl.when(dst == x)
                def _():
                    own[f, rows(r)] = half

                @pl.when(dst != x)
                def _():
                    xsend[f, dst, rows(r)] = half.astype(BF16)
                    to_x(f, dst, r).start()

    def combine(k, i, r):
        f = 2 * ((x + 4 - i) % 2 + 2 * k) + i // 2
        total = own[f, rows(r)]
        for dx in range(1, X):
            src = (x + dx) % 4
            arrived(xrecv.at[f, src, rows(r)], xrs.at[f, src, r])
            total += xrecv[f, src, rows(r)].astype(F32)

        @pl.when(f == z)
        def _():
            own[f, rows(r)] = total

        @pl.when(f != z)
        def _():
            zsend[f, rows(r)] = total.astype(BF16)
            to_z(f, r).start()

    def use_down(q, r):
        if r == 0:
            for d in (0, 1) if q == 0 else (q + 1,):
                from_sibling(DOWN, d)
                from_sibling(DOWN2, d)
        for k in range(2):
            project(k, pair(q), r)
            if q:
                combine(k, pair(q - 1), r)

    deal(GATE)
    deal(UP)
    for m in (DOWN, DOWN2, FIRST, SECOND):
        spread(m)
    keep_tokens()
    gacc[...] = jnp.zeros_like(gacc)
    uacc[...] = jnp.zeros_like(uacc)
    circulate(GATE, 0)
    deal_tokens(0)
    circulate(UP, 0)
    deal_tokens(1)
    token_step(0, 0)
    circulate(GATE, -1)
    circulate(GATE, 1)
    down_step(0)
    circulate(UP, -1)
    circulate(UP, 1)
    token_step(1, 0)
    token_step(2, 0)
    for m in (GATE, UP):
        circulate(m, 2)
    down_step(1)
    token_step(3, 0)
    token_step(0, 1)
    tokens_kept()
    for m in (GATE, UP):
        weights_from_sibling(m)
    for d in (0, 1, 7, 2, 6):
        multiply((z + d) % 8, 0)
    down_step(2)
    token_step(4, 0)
    for d in (3, 5, 4):
        multiply((z + d) % 8, 0)
    pass_hidden(0)
    token_step(1, 1)
    down_step(3)
    token_step(2, 1)
    hidden_here(0)
    use_down(0, 0)
    down_step(4)
    adapters(0)
    use_down(1, 0)
    token_step(3, 1)
    for d in (0, 1, 7):
        multiply((z + d) % 8, 1)
    adapters(1)
    use_down(2, 0)
    for d in (2, 6, 3, 5):
        multiply((z + d) % 8, 1)
    token_step(4, 1)
    multiply((z + 4) % 8, 1)
    pass_hidden(1)
    adapters(2)
    use_down(3, 0)
    adapters(3)
    for k in range(2):
        combine(k, pair(3), 0)
    adapters(4)
    hidden_here(1)
    use_down(0, 1)
    for d in range(5):
        from_sibling(FIRST, d)
        from_sibling(SECOND, d)
    low_terms()
    use_down(1, 1)
    low_over_x()
    use_down(2, 1)
    low_over_z()
    use_down(3, 1)
    for k in range(2):
        combine(k, pair(3), 1)

    for m in range(6):
        if m <= UP:
            sent(bufs[m].at[pl.ds(0, 2)], gs.at[m])
            sent(bufs[m].at[pl.ds(0, 6)], rs.at[m])
            sent(bufs[m].at[pl.ds(0, 8)], ss.at[m])
            continue
        spread(m, go=False)
        if m == SECOND:
            onward, across = bbuf.at[0, pl.ds(0, 7)], bbuf.at[0]
        elif m >= DOWN:
            onward, across = dbuf.at[pl.ds(0, 2), pl.ds(0, 7), rows(0)], dbuf.at[pl.ds(0, 2), :, rows(0)]
        else:
            onward, across = bufs[m].at[pl.ds(0, 2), pl.ds(0, 7)], bufs[m].at[pl.ds(0, 2)]
        sent(onward, rs.at[m])
        sent(across, ss.at[m])
    sent(tok.at[0, pl.ds(0, 3), 0], ts)
    for k in range(2):
        pl.when(jnp.logical_not(held(k)))(lambda k=k: sent(tok.at[k, pl.ds(0, 7)], tz.at[k]))
        pl.when(jnp.logical_not(own_hid & (k == x % 2)))(lambda k=k: sent(hs.at[k], hss.at[k]))
    sent(lxr.at[pl.ds(0, 3)], lxss)
    sent(lzr.at[pl.ds(0, 7)], lzss)
    sent(lows.at[pl.ds(0, 96)], lbss)
    sent(xsend.at[:, pl.ds(0, 3)], xss)

    for dx in range(1, X):
        src = (x + dx) % 4
        arrived(lows.at[quarter(src)], lbrs.at[src])
    low_rounded = lows[...]
    lora = []
    for b in range(2):
        s = chosen[b]
        r = s // 16
        xs, i, u = s // 8, (s // 2) % 4, s % 2
        ys = 2 * i + (r + bx) % 2
        lora.append(jnp.dot(low_rounded[:, b * RANK:(b + 1) * RANK], bbuf[xs % 2, ys, u], preferred_element_type=F32))

    total = own[z]
    for dz in range(1, Z):
        src = (z + dz) % 8
        for r in range(2):
            arrived(zrecv.at[src, rows(r)], zrs.at[src, r])
        total += zrecv[src].astype(F32)
    total += 2.0 * jnp.concatenate(lora, axis=0)
    row = lax.broadcasted_iota(jnp.int32, (2 * BLOCK, BLOCK), 0)
    limit = jnp.where(row < BLOCK, live[role * 2], BLOCK + live[role * 2 + 1])
    mixed = jnp.where(row < limit, total, 0.0).astype(BF16)

    stays = (tx == x) & (bx == x)
    back = copy(fsend, frecv, fss, frs, place(tx, yh * 2 + bx % 2, z, bx // 2))

    @pl.when(stays)
    def _():
        out[...] = mixed

    @pl.when(jnp.logical_not(stays))
    def _():
        fsend[...] = mixed
        back.start()

    sent(zsend.at[pl.ds(0, 7)], zss)

    @pl.when(jnp.logical_not(stays))
    def _():
        arrived(frecv, frs)
        out[...] = frecv[...]
        sent(fsend, fss)


def local(tokens, gate, up, down, first, second, slots, live):
    dma = pltpu.SemaphoreType.DMA
    smem = pl.BlockSpec(memory_space=pltpu.SMEM)
    hbm = pl.BlockSpec(memory_space=pl.ANY)
    return pl.pallas_call(
        kernel,
        out_shape=jax.ShapeDtypeStruct((256, 128), BF16),
        in_specs=[smem, smem] + [hbm] * 6,
        out_specs=pl.BlockSpec(memory_space=pltpu.VMEM),
        scratch_shapes=[
            pltpu.VMEM((16, 256, 256), BF16),
            pltpu.VMEM((16, 256, 256), BF16),
            pltpu.VMEM((4, 8, 256, 256), BF16),
            pltpu.VMEM((4, 8, 2, RANK, 256), BF16),
            pltpu.VMEM((2, 8, 2, RANK, 128), BF16),
            pltpu.VMEM((2, 8, 2, 256, 256), BF16),
            pltpu.VMEM((2, 256, 256), F32),
            pltpu.VMEM((2, 256, 256), F32),
            pltpu.VMEM((2, 256, 256), BF16),
            pltpu.VMEM((2, 256, 256), BF16),
            pltpu.VMEM((8, 256, 128), F32),
            pltpu.VMEM((8, 4, 256, 128), BF16),
            pltpu.VMEM((8, 4, 256, 128), BF16),
            pltpu.VMEM((8, 256, 128), BF16),
            pltpu.VMEM((8, 256, 128), BF16),
            pltpu.VMEM((128, 128), F32),
            pltpu.VMEM((4, 32, 128), F32),
            pltpu.VMEM((32, 128), F32),
            pltpu.VMEM((8, 32, 128), F32),
            pltpu.VMEM((128, 128), BF16),
            pltpu.VMEM((256, 128), BF16),
            pltpu.VMEM((256, 128), BF16),
            dma((6, 2)),
            dma((6, 2, 8)),
            dma((2,)),
            dma((6,)),
            dma((6,)),
            dma((6, 2, 8)),
            dma(()),
            dma((2, 8, 2, 2)),
            dma((2,)),
            dma(()),
            dma((2,)),
            dma((2, 2)),
            dma(()),
            dma((8, 4, 2)),
            dma(()),
            dma((8, 2)),
            dma(()),
            dma((4,)),
            dma(()),
            dma((8,)),
            dma(()),
            dma((4,)),
            dma(()),
            dma(()),
        ],
        compiler_params=pltpu.CompilerParams(
            collective_id=0, has_side_effects=True, vmem_limit_bytes=60 << 20
        ),
        name="swiglu_mesh",
    )(slots, live, tokens, gate, up, down, first, second)


def solution(mesh):
    in_specs = (
        P("narrow", None),
        P("narrow", "wide"),
        P("narrow", "wide"),
        P("wide", "narrow"),
        P("narrow", None, "wide"),
        P("narrow", None, "wide"),
        P(),
        P(),
    )
    return jax.shard_map(local, mesh=mesh, in_specs=in_specs, out_specs=P("narrow", "wide"), check_vma=False)
```

```python
import jax
import jax.numpy as jnp
from jax import lax
from jax.experimental import pallas as pl
from jax.experimental.pallas import tpu as pltpu
from jax.sharding import PartitionSpec as P

MESH = pl.DeviceIdType.MESH
BF16, F32 = jnp.bfloat16, jnp.float32
BLOCK = 128
RANK = 64
X, Y, Z = 4, 8, 8
GATE, UP, FIRST, SECOND, DOWN, DOWN2 = range(6)


def place(x, y, z, core):
    return {"narrow": x * 4 + y // 2, "wide": z * 4 + (y % 2) * 2 + core}


def kernel(
    slots, live, tokens, gate, up, down, first, second, out,
    gbuf, ubuf, dbuf, abuf, bbuf, tok, gacc, uacc, hs, hid,
    own, xsend, xrecv, zsend, zrecv, lxs, lxr, lzs, lzr, lows, fsend, frecv,
    ws, wr, gs, rs, ss, sr, ts, tr, tz, tn, hss, hr, xss, xrs, zss, zrs, lxss, lxrs, lzss, lzrs, lbss, lbrs, fss, frs,
):
    n = lax.axis_index("narrow")
    w = lax.axis_index("wide")
    x, yh = n // 4, n % 4
    z, yl, core = w // 4, (w // 2) % 2, w % 2
    y = yh * 2 + yl
    tx = yl + 2 * core
    role = tx * 4 + yh
    bx = (x + 4 - z // 2) % 4

    def copy(src, dst, send, recv, dev):
        return pltpu.make_async_remote_copy(
            src_ref=src, dst_ref=dst, send_sem=send, recv_sem=recv, device_id=dev, device_id_type=MESH
        )

    def arrived(dst, recv):
        copy(dst, dst, recv, recv, place(x, y, z, 1 - core)).wait_recv()

    def sent(src, send):
        copy(src, src, send, send, place(x, y, z, 1 - core)).wait_send()

    barrier = pltpu.get_barrier_semaphore()
    partners = [place(x, (y + dy) % 8, z, (core + dc) % 2) for dy in range(Y) for dc in range(2) if dy or dc]
    for dx in range(1, X):
        for dc in range(2):
            for dy in range(2):
                partners.append(place((x + dx) % 4, yh * 2 + (yl + dy) % 2, z, (core + dc) % 2))
    for dz in range(1, Z):
        partners.append(place(x, y, (z + dz) % 8, core))
    for partner in partners:
        pl.semaphore_signal(barrier, inc=1, device_id=partner, device_id_type=MESH)
    own_hid = (yh == x) & (yl == x % 2) & (core == x // 2)
    for p in range(2):
        @pl.when(jnp.logical_not(own_hid & (p == 1 - yl)))
        def _():
            pl.semaphore_signal(barrier, inc=1, device_id=place(tx, 2 * x + 1 - p, z, yh // 2), device_id_type=MESH)
    pl.semaphore_wait(barrier, len(partners) + 2 - jnp.where(own_hid, 1, 0))

    bufs = (gbuf, ubuf, abuf, bbuf)

    def chunk(m, c, k, ys):
        if m == SECOND:
            return bbuf.at[c, ys, k]
        if m >= DOWN:
            return dbuf.at[c + 2 * k, ys, pl.ds((m - DOWN) * 128, 128)]
        return bufs[m].at[c + 2 * k, ys]

    def spread_one(m, e, dx, dy, src, dst, recv, go):
        stays = (dx == x) & (x % 2 == core) & (dy == y)
        if go:
            @pl.when(stays)
            def _():
                pltpu.make_async_copy(src, dst, recv).start()

            @pl.when(jnp.logical_not(stays))
            def _():
                copy(src, dst, ws.at[m, e], recv, place(dx, dy, z, x % 2)).start()
        else:
            @pl.when(jnp.logical_not(stays))
            def _():
                sent(src, ws.at[m, e])

    def spread(m, go=True):
        k = x // 2
        for e in range(2):
            if m == SECOND:
                dy = yh * 2 + (yl + k) % 2
                spread_one(m, e, (tx + z // 2) % 4, dy, second.at[e], bbuf.at[x % 2, dy, e], wr.at[m, e, dy], go)
                continue
            if m >= DOWN:
                h = (m - DOWN) * 128
                src = down.at[pl.ds(e * 256 + h, 128), :]
                dst = dbuf.at[x, y, pl.ds(h, 128)]
                spread_one(m, e, 2 * core + e, y, src, dst, wr.at[m, k, y], go)
                continue
            src = first.at[:, :, pl.ds(e * 256, 256)]
            spread_one(m, e, 2 * core + e, y, src, bufs[m].at[x, y], wr.at[m, k, y], go)

    def ring_step(m, d):
        for k in range(2):
            for way in (1, -1):
                reach = 4 if way == 1 - 2 * k else 3
                if d > reach or (d == 0 and way == -1):
                    continue
                ys = (y - way * d + 8) % 8
                ref, recv = chunk(m, core, k, ys), wr.at[m, k, ys]
                arrived(ref, recv)
                for onward in (1, -1) if d == 0 else (way,):
                    if d < reach:
                        copy(ref, ref, rs.at[m], recv, place(x, (y + onward + 8) % 8, z, core)).start()
                copy(ref, ref, ss.at[m], sr.at[m, k, ys], place(x, y, z, 1 - core)).start()

    def from_sibling(m, d):
        for k in range(2):
            for ys in ((y + 8 - d) % 8, (y + d) % 8)[:1 if d in (0, 4) else 2]:
                arrived(chunk(m, 1 - core, k, ys), sr.at[m, k, ys])

    def deal(m):
        src = (gate, up)[m]
        for e in range(2):
            to = place(x, 2 * (2 * core + e) + 1 - yl, z, yh // 2)
            copy(src.at[:, pl.ds(e * 256, 256)], bufs[m].at[4 * x + yh], gs.at[m], wr.at[m, yh % 2, x], to).start()

    def circulate(m, dx):
        xs = (x + dx + 4) % 4
        for k in range(2):
            ref, recv = bufs[m].at[4 * xs + 2 * core + k], wr.at[m, k, xs]
            arrived(ref, recv)
            for way in (1, -1):
                if dx == 0 or (dx == -way and way == 1 - 2 * k):
                    copy(ref, ref, rs.at[m], recv, place((x + way + 4) % 4, y, z, core)).start()
            copy(ref, ref, ss.at[m], sr.at[m, k, xs], place(x, y, z, 1 - core)).start()

    def weights_from_sibling(m):
        for xs in range(4):
            for k in range(2):
                arrived(bufs[m].at[4 * xs + 2 * (1 - core) + k], sr.at[m, k, xs])

    def rows(r):
        return pl.ds(r * BLOCK, BLOCK)

    def deal_tokens(r):
        src = tokens.at[rows(r), pl.ds(pl.multiple_of(z * 512 + core * 256, 256), 256)]
        for step in range(1, 4):
            to = place(x, (y + step * (2 * yl - 1) + 8) % 8, z, yh // 2)
            copy(src, tok.at[yh % 2, z, core, rows(r)], ts, tr.at[yh % 2, z, core, r], to).start()

    def held(k):
        return yh == 2 * core + k

    def keep_tokens():
        @pl.when(core == yh // 2)
        def _():
            for part in range(16):
                src = tokens.at[:, pl.ds(part * 256, 256)]
                pltpu.make_async_copy(src, tok.at[yh % 2, part // 2, part % 2], tn).start()

    def tokens_kept():
        @pl.when(core == yh // 2)
        def _():
            pltpu.make_async_copy(tok.at[yh % 2], tok.at[yh % 2], tn).wait()

    def token_step(d, r):
        for k in range(2):
            @pl.when(jnp.logical_not(held(k)))
            def _():
                for way in (1, -1):
                    reach = 4 if way == 1 - 2 * k else 3
                    if d > reach or (d == 0 and way == -1):
                        continue
                    zs = (z - way * d + 8) % 8
                    for h in range(2):
                        ref, recv = tok.at[k, zs, h, rows(r)], tr.at[k, zs, h, r]
                        arrived(ref, recv)
                        for onward in (1, -1) if d == 0 else (way,):
                            if d < reach or d == 0:
                                copy(ref, ref, tz.at[k], recv, place(x, y, (z + onward + 8) % 8, core)).start()

    def multiply(zs, r):
        for k in range(2):
            for m, acc in ((GATE, gacc), (UP, uacc)):
                total = acc[k, rows(r)]
                for h in range(2):
                    total += jnp.dot(tok[k, zs, h, rows(r)], bufs[m][2 * zs + h], preferred_element_type=F32)
                acc[k, rows(r)] = total

    def pass_hidden(r):
        for k in range(2):
            hs[k, rows(r)] = (jax.nn.silu(gacc[k, rows(r)]) * uacc[k, rows(r)]).astype(BF16)
            stays = own_hid & (k == x % 2)
            src, dst, recv = hs.at[k, rows(r)], hid.at[1 - yl, rows(r)], hr.at[1 - yl, r]

            @pl.when(stays)
            def _():
                pltpu.make_async_copy(src, dst, recv).start()

            @pl.when(jnp.logical_not(stays))
            def _():
                copy(src, dst, hss.at[k], recv, place(yh, 4 * core + 2 * k + x % 2, z, x // 2)).start()

    def adapters(d):
        ring_step(FIRST, d)
        ring_step(SECOND, d)

    def down_step(d):
        ring_step(DOWN, d)
        ring_step(DOWN2, d)

    def hidden_here(r):
        for p in range(2):
            arrived(hid.at[p, rows(r)], hr.at[p, r])

    chosen = [slots[role * 2 + b] for b in range(2)]

    def quarter(i):
        return pl.ds(pl.multiple_of(i * 32, 32), 32)

    def low_x(dst):
        return copy(lxs.at[quarter(dst)], lxr.at[x], lxss, lxrs.at[x], place(dst, y, z, core))

    def low_z(dz):
        return copy(lzs, lzr.at[z], lzss, lzrs.at[z], place(x, y, (z + dz) % 8, core))

    def low_back(dst):
        part = lows.at[quarter(x)]
        return copy(part, part, lbss, lbrs.at[x], place(dst, y, z, core))

    def low_terms():
        low = []
        for b in range(2):
            s = chosen[b]
            part = jnp.zeros((BLOCK, RANK), F32)
            for p in range(2):
                row = (s // 8) * 16 + ((s // 2) % 4) * 4 + 2 * p + s % 2
                part += lax.dot_general(
                    hid[p, b * BLOCK:(b + 1) * BLOCK, :],
                    abuf[row // 16, (row // 2) % 8, row % 2],
                    (((1,), (1,)), ((), ())),
                    preferred_element_type=F32,
                )
            low.append(part)
        lxs[...] = jnp.concatenate(low, axis=1)
        for dx in range(1, X):
            low_x((x + dx) % 4).start()

    def low_over_x():
        total = lxs[quarter(x)]
        for dx in range(1, X):
            src = (x + dx) % 4
            arrived(lxr.at[src], lxrs.at[src])
            total += lxr[src]
        lzs[...] = total
        for dz in range(1, Z):
            low_z(dz).start()

    def low_over_z():
        total = lzs[...]
        for dz in range(1, Z):
            src = (z + dz) % 8
            arrived(lzr.at[src], lzrs.at[src])
            total += lzr[src]
        lows[quarter(x)] = total.astype(BF16)
        for dx in range(1, X):
            low_back((x + dx) % 4).start()

    def pair(q):
        return (yh + (0, 2 * yl - 1, 1 - 2 * yl, 2)[q] + 4) % 4

    def to_x(f, dst, r):
        return copy(xsend.at[f, dst, rows(r)], xrecv.at[f, x, rows(r)], xss, xrs.at[f, x, r], place(dst, y, z, core))

    def to_z(f, r):
        return copy(zsend.at[f, rows(r)], zrecv.at[z, rows(r)], zss, zrs.at[z, r], place(x, y, f, core))

    def project(k, i, r):
        for c in range(2):
            xs = c + 2 * k
            part = jnp.dot(hid[0, rows(r)], dbuf[xs, 2 * i], preferred_element_type=F32)
            part += jnp.dot(hid[1, rows(r)], dbuf[xs, 2 * i + 1], preferred_element_type=F32)
            f = 2 * xs + i // 2
            for h in range(2):
                dst = (i % 2 + 2 * h + xs) % 4
                half = part[:, h * 128:(h + 1) * 128]

                @pl.when(dst == x)
                def _():
                    own[f, rows(r)] = half

                @pl.when(dst != x)
                def _():
                    xsend[f, dst, rows(r)] = half.astype(BF16)
                    to_x(f, dst, r).start()

    def combine(k, i, r):
        f = 2 * ((x + 4 - i) % 2 + 2 * k) + i // 2
        total = own[f, rows(r)]
        for dx in range(1, X):
            src = (x + dx) % 4
            arrived(xrecv.at[f, src, rows(r)], xrs.at[f, src, r])
            total += xrecv[f, src, rows(r)].astype(F32)

        @pl.when(f == z)
        def _():
            own[f, rows(r)] = total

        @pl.when(f != z)
        def _():
            zsend[f, rows(r)] = total.astype(BF16)
            to_z(f, r).start()

    def use_down(q, r):
        if r == 0:
            for d in (0, 1) if q == 0 else (q + 1,):
                from_sibling(DOWN, d)
                from_sibling(DOWN2, d)
        for k in range(2):
            project(k, pair(q), r)
            if q:
                combine(k, pair(q - 1), r)

    deal(GATE)
    deal(UP)
    for m in (DOWN, DOWN2, FIRST, SECOND):
        spread(m)
    keep_tokens()
    gacc[...] = jnp.zeros_like(gacc)
    uacc[...] = jnp.zeros_like(uacc)
    circulate(GATE, 0)
    deal_tokens(0)
    circulate(UP, 0)
    deal_tokens(1)
    token_step(0, 0)
    circulate(GATE, -1)
    circulate(GATE, 1)
    down_step(0)
    circulate(UP, -1)
    circulate(UP, 1)
    token_step(1, 0)
    token_step(2, 0)
    for m in (GATE, UP):
        circulate(m, 2)
    down_step(1)
    token_step(3, 0)
    token_step(0, 1)
    tokens_kept()
    for m in (GATE, UP):
        weights_from_sibling(m)
    for d in (0, 1, 7, 2, 6):
        multiply((z + d) % 8, 0)
    down_step(2)
    token_step(4, 0)
    for d in (3, 5, 4):
        multiply((z + d) % 8, 0)
    pass_hidden(0)
    token_step(1, 1)
    down_step(3)
    token_step(2, 1)
    hidden_here(0)
    use_down(0, 0)
    down_step(4)
    adapters(0)
    use_down(1, 0)
    token_step(3, 1)
    for d in (0, 1, 7):
        multiply((z + d) % 8, 1)
    adapters(1)
    use_down(2, 0)
    for d in (2, 6, 3, 5):
        multiply((z + d) % 8, 1)
    token_step(4, 1)
    multiply((z + 4) % 8, 1)
    pass_hidden(1)
    adapters(2)
    use_down(3, 0)
    adapters(3)
    for k in range(2):
        combine(k, pair(3), 0)
    adapters(4)
    hidden_here(1)
    use_down(0, 1)
    for d in range(5):
        from_sibling(FIRST, d)
        from_sibling(SECOND, d)
    low_terms()
    use_down(1, 1)
    low_over_x()
    use_down(2, 1)
    use_down(3, 1)
    low_over_z()
    for k in range(2):
        combine(k, pair(3), 1)

    for m in range(6):
        if m <= UP:
            sent(bufs[m].at[pl.ds(0, 2)], gs.at[m])
            sent(bufs[m].at[pl.ds(0, 6)], rs.at[m])
            sent(bufs[m].at[pl.ds(0, 8)], ss.at[m])
            continue
        spread(m, go=False)
        if m == SECOND:
            onward, across = bbuf.at[0, pl.ds(0, 7)], bbuf.at[0]
        elif m >= DOWN:
            onward, across = dbuf.at[pl.ds(0, 2), pl.ds(0, 7), rows(0)], dbuf.at[pl.ds(0, 2), :, rows(0)]
        else:
            onward, across = bufs[m].at[pl.ds(0, 2), pl.ds(0, 7)], bufs[m].at[pl.ds(0, 2)]
        sent(onward, rs.at[m])
        sent(across, ss.at[m])
    sent(tok.at[0, pl.ds(0, 3), 0], ts)
    for k in range(2):
        pl.when(jnp.logical_not(held(k)))(lambda k=k: sent(tok.at[k, pl.ds(0, 7)], tz.at[k]))
        pl.when(jnp.logical_not(own_hid & (k == x % 2)))(lambda k=k: sent(hs.at[k], hss.at[k]))
    sent(lxr.at[pl.ds(0, 3)], lxss)
    sent(lzr.at[pl.ds(0, 7)], lzss)
    sent(lows.at[pl.ds(0, 96)], lbss)
    sent(xsend.at[:, pl.ds(0, 3)], xss)

    for dx in range(1, X):
        src = (x + dx) % 4
        arrived(lows.at[quarter(src)], lbrs.at[src])
    low_rounded = lows[...]
    lora = []
    for b in range(2):
        s = chosen[b]
        r = s // 16
        xs, i, u = s // 8, (s // 2) % 4, s % 2
        ys = 2 * i + (r + bx) % 2
        lora.append(jnp.dot(low_rounded[:, b * RANK:(b + 1) * RANK], bbuf[xs % 2, ys, u], preferred_element_type=F32))

    total = own[z]
    for dz in range(1, Z):
        src = (z + dz) % 8
        for r in range(2):
            arrived(zrecv.at[src, rows(r)], zrs.at[src, r])
        total += zrecv[src].astype(F32)
    total += 2.0 * jnp.concatenate(lora, axis=0)
    row = lax.broadcasted_iota(jnp.int32, (2 * BLOCK, BLOCK), 0)
    limit = jnp.where(row < BLOCK, live[role * 2], BLOCK + live[role * 2 + 1])
    mixed = jnp.where(row < limit, total, 0.0).astype(BF16)

    stays = (tx == x) & (bx == x)
    back = copy(fsend, frecv, fss, frs, place(tx, yh * 2 + bx % 2, z, bx // 2))

    @pl.when(stays)
    def _():
        out[...] = mixed

    @pl.when(jnp.logical_not(stays))
    def _():
        fsend[...] = mixed
        back.start()

    sent(zsend.at[pl.ds(0, 7)], zss)

    @pl.when(jnp.logical_not(stays))
    def _():
        arrived(frecv, frs)
        out[...] = frecv[...]
        sent(fsend, fss)


def local(tokens, gate, up, down, first, second, slots, live):
    dma = pltpu.SemaphoreType.DMA
    smem = pl.BlockSpec(memory_space=pltpu.SMEM)
    hbm = pl.BlockSpec(memory_space=pl.ANY)
    return pl.pallas_call(
        kernel,
        out_shape=jax.ShapeDtypeStruct((256, 128), BF16),
        in_specs=[smem, smem] + [hbm] * 6,
        out_specs=pl.BlockSpec(memory_space=pltpu.VMEM),
        scratch_shapes=[
            pltpu.VMEM((16, 256, 256), BF16),
            pltpu.VMEM((16, 256, 256), BF16),
            pltpu.VMEM((4, 8, 256, 256), BF16),
            pltpu.VMEM((4, 8, 2, RANK, 256), BF16),
            pltpu.VMEM((2, 8, 2, RANK, 128), BF16),
            pltpu.VMEM((2, 8, 2, 256, 256), BF16),
            pltpu.VMEM((2, 256, 256), F32),
            pltpu.VMEM((2, 256, 256), F32),
            pltpu.VMEM((2, 256, 256), BF16),
            pltpu.VMEM((2, 256, 256), BF16),
            pltpu.VMEM((8, 256, 128), F32),
            pltpu.VMEM((8, 4, 256, 128), BF16),
            pltpu.VMEM((8, 4, 256, 128), BF16),
            pltpu.VMEM((8, 256, 128), BF16),
            pltpu.VMEM((8, 256, 128), BF16),
            pltpu.VMEM((128, 128), F32),
            pltpu.VMEM((4, 32, 128), F32),
            pltpu.VMEM((32, 128), F32),
            pltpu.VMEM((8, 32, 128), F32),
            pltpu.VMEM((128, 128), BF16),
            pltpu.VMEM((256, 128), BF16),
            pltpu.VMEM((256, 128), BF16),
            dma((6, 2)),
            dma((6, 2, 8)),
            dma((2,)),
            dma((6,)),
            dma((6,)),
            dma((6, 2, 8)),
            dma(()),
            dma((2, 8, 2, 2)),
            dma((2,)),
            dma(()),
            dma((2,)),
            dma((2, 2)),
            dma(()),
            dma((8, 4, 2)),
            dma(()),
            dma((8, 2)),
            dma(()),
            dma((4,)),
            dma(()),
            dma((8,)),
            dma(()),
            dma((4,)),
            dma(()),
            dma(()),
        ],
        compiler_params=pltpu.CompilerParams(
            collective_id=0, has_side_effects=True, vmem_limit_bytes=60 << 20
        ),
        name="swiglu_mesh",
    )(slots, live, tokens, gate, up, down, first, second)


def solution(mesh):
    in_specs = (
        P("narrow", None),
        P("narrow", "wide"),
        P("narrow", "wide"),
        P("wide", "narrow"),
        P("narrow", None, "wide"),
        P("narrow", None, "wide"),
        P(),
        P(),
    )
    return jax.shard_map(local, mesh=mesh, in_specs=in_specs, out_specs=P("narrow", "wide"), check_vma=False)
```
